1024 devices in a mesh: expert: 16 (over z_lo, core), replica: 16 (over y, x), micro: 4 (over z_hi).
Axes of the slice: x: 4, y: 4, z: 32 (z_hi: 4, z_lo: 8; z = z_hi * 8 + z_lo), core: 2. Of those that a mesh axis runs over, the one named last changes fastest.
Arguments:
- grad_rows: bfloat16 [131072, 3584], P(('expert', 'replica', 'micro')), may hold values from -0.19921875 to 0.19921875
- routing: int32 [131072, 1], P(('expert', 'replica', 'micro')), may hold values from 0 to 15; in each aligned block of 128 rows (0 to 127, 128 to 255, ...) at most 10 rows name the same one
- route_weight: float32 [131072, 1], P(('expert', 'replica', 'micro')), may hold values from 0.05 to 1
- saved_hidden: bfloat16 [163840, 1024], P(('expert', 'replica', 'micro')), may hold values from -24 to 24
Outputs:
- grad_weight: float32 [16, 1024, 3584], P('expert', 'replica', 'micro')
The draws below stay inside these ranges and needn't reach their ends.
Inputs may be any that keep to these rules, and one draw needn't show every extreme that they name: `routing`: the tokens of one device name one expert in at most 10 rows; in every draw some device names some expert in exactly 10 rows.
All inputs are finite; a program needn't handle non-finite values.
Results may differ from the reference program's by a relative error of at most 0.015.
Values may be sent and summed in bfloat16 or wider, within the bound.
No kernel may reach another device: no remote copies, remote signals or barrier semaphores. Data moves between devices by JAX's collectives and lax.ppermute only.
A program may use at most 64 MiB of HBM per device.

```python
import math
import jax
import jax.numpy as jnp
import numpy as np
from jax import lax

D_WIN = 3584
FF = 1024
TOK_DEV = 128
ROUTES = 1
EXPERTS = 16
CAP = 10
SLOTS = 160
TOKENS = 131072
HROWS = 163840
N_EXPERT = 16
N_REPLICA = 16
N_MICRO = 4


def with_spikes(values, own_key, source, target, blocks, factor):
    def block_of(axis_at):
        return (jnp.arange(values.shape[axis_at]) // (values.shape[axis_at] // blocks)).reshape((-1,) + (1,) * (values.ndim - 1 - axis_at))

    near = jax.random.permutation(own_key, blocks)[block_of(target)]
    other_side = (block_of(target) + blocks // 2) % blocks
    return jnp.where((block_of(source) == near) | (block_of(source) == other_side), factor * values, values)


def block_levels(stream_key, extent, pieces, low, largest):
    gain = 1.0
    for axis_at, parts in pieces:
        steps = jax.random.uniform(jax.random.fold_in(jax.random.fold_in(stream_key, 6), axis_at), (parts,), jnp.float32, low / len(pieces), largest / len(pieces))
        gain = gain * jnp.repeat(jnp.exp(steps), extent[axis_at] // parts).reshape((-1,) + (1,) * (len(extent) - 1 - axis_at))
    return gain


def deal_out(own_key, own, number, rows, number_of, top, bound, skew):
    ranking = jax.random.permutation(own_key, number_of)
    crowded, ordinary = shares(number_of, rows * top, bound, skew, True), shares(number_of, rows * top, bound, skew, False)
    places = jnp.arange(number_of)

    def named(sizes, offset_by):
        used = int((sizes > 0).sum())
        fixed = max(1, used // 4)
        moved = fixed + (places - fixed + offset_by * (used - fixed)) % max(1, number_of - fixed)
        return jnp.zeros((number_of,), jnp.int32).at[ranking[jnp.where(places < fixed, places, moved)]].set(jnp.asarray(sizes, jnp.int32))

    sizes = jnp.where(number % 4 == 0, named(crowded, number // 4), named(ordinary, number - number // 4 - 1))
    mixed = jax.random.permutation(jax.random.fold_in(own, 3), number_of)
    source_of, sink = mixed[0:number_of // 2 * 2:2], mixed[1:number_of // 2 * 2:2]
    slack = jnp.minimum(sizes[source_of] - 1, bound - sizes[sink]) // 2
    slack = jnp.where((source_of == ranking[0]) | (sink == ranking[0]) | (sizes[sink] == 0), 0, jnp.maximum(slack, 0))
    moved = jax.random.randint(jax.random.fold_in(own, 4), (number_of // 2,), 0, 1 << 20) % (slack + 1)
    sizes = sizes.at[source_of].add(-moved).at[sink].add(moved)
    labels = jnp.searchsorted(jnp.cumsum(sizes), jnp.arange(rows * top), side="right").astype(jnp.int32)
    listing = labels.reshape(top, rows).T
    listing = listing[jax.random.permutation(jax.random.fold_in(own, 1), rows)]
    offset_by = jax.random.randint(jax.random.fold_in(own, 2), (rows, 1), 0, top)
    return jnp.take_along_axis(listing, (jnp.arange(top)[None, :] + offset_by) % top, axis=1)


def shares(amount, total, limit, lean, full):
    weights = [(1 << 20) // math.isqrt(rank ** lean) + 1 for rank in range(1, amount + 1)]
    largest = limit if full else min(limit, max(-(-total // amount), total * weights[0] // sum(weights)))
    least = 1 if total - largest >= amount - 1 else 0
    counts, rest = [largest] + [least] * (amount - 1), total - largest - least * (amount - 1)
    while rest > 0:
        movable = [i for i in range(1, amount) if counts[i] < largest] or [i for i in range(1, amount) if counts[i] < limit]
        pool, remaining = sum([weights[i] for i in movable]), rest
        for i in movable:
            extra = min(limit - counts[i], max(1, remaining * weights[i] // pool), rest)
            counts[i] = counts[i] + extra
            rest = rest - extra
    return np.array(counts)


def noise(stream_key, dims, scale, most, cuts=(), held_as=jnp.bfloat16):
    loudness = block_levels(stream_key, dims, cuts, -0.22, 0.18) if cuts else 1.0
    result = jax.random.normal(stream_key, dims, jnp.float32) * scale * loudness
    return jnp.minimum(jnp.maximum(result, -most), most).astype(held_as)


def noise_with(stream_key, dims, width, most, pieces, heavy, held_as=jnp.bfloat16):
    drawn = width * jax.random.normal(stream_key, dims, jnp.float32)
    if pieces:
        drawn = drawn * block_levels(stream_key, dims, pieces, -0.22, 0.18)
    return jnp.clip(with_spikes(drawn, jax.random.fold_in(stream_key, 3), *heavy), -most, most).astype(held_as)


def setup_inputs(seed: int = 0) -> dict:
    key_list = jax.random.split(jax.random.key(seed), 5)
    grad_rows = noise(key_list[0], (TOKENS, D_WIN), 0.03, 0.19921875, ((0, 1024),))
    routing_keys = jax.random.split(jax.random.fold_in(key_list[1], 1), TOKENS // TOK_DEV)
    routing_turns = jax.random.permutation(jax.random.fold_in(key_list[1], 3), TOKENS // TOK_DEV)
    routing = jax.vmap(lambda own, number: deal_out(jax.random.fold_in(key_list[1], 2), own, number, TOK_DEV, EXPERTS, ROUTES, CAP, 2))(routing_keys, routing_turns).reshape((TOKENS, ROUTES))
    route_weight = jnp.clip(jnp.exp(math.log(1.0) - 2.9957323 * jax.random.uniform(key_list[2], (TOKENS, ROUTES), jnp.float32) ** block_levels(key_list[2], (TOKENS, ROUTES), ((0, 1024),), -0.2, 0.2)), 0.05, 1.0)
    saved_hidden = noise_with(key_list[3], (HROWS, FF), 1.0, 24.0, ((0, 1024),), (0, 1, 1024, 6.0))
    return dict(grad_rows=grad_rows, routing=routing, route_weight=route_weight, saved_hidden=saved_hidden)


def reference(grad_rows, routing, route_weight, saved_hidden):
    grad_blocks = grad_rows.reshape(N_EXPERT, N_REPLICA, N_MICRO, TOK_DEV, D_WIN)
    targets = routing[:, 0].reshape(N_EXPERT, N_REPLICA, N_MICRO, TOK_DEV)
    weights = route_weight[:, 0].reshape(N_EXPERT, N_REPLICA, N_MICRO, TOK_DEV)
    member = (targets[..., None] == jnp.arange(EXPERTS, dtype=jnp.int32)).astype(jnp.int32)
    running = jnp.cumsum(member, axis=3).astype(jnp.int32) - 1
    positions = jnp.sum(member * running, axis=-1).astype(jnp.int32)
    hidden_blocks = saved_hidden.reshape(N_EXPERT, N_REPLICA, N_MICRO * SLOTS, FF)
    source_ids = jnp.arange(N_EXPERT, dtype=jnp.int32)[:, None, None]
    micro_ids = jnp.arange(N_MICRO, dtype=jnp.int32)[None, :, None]

    def one_block(expert_id, replica_id):
        source_rows = lax.dynamic_index_in_dim(grad_blocks, replica_id, 1, keepdims=False)
        source_weights = lax.dynamic_index_in_dim(weights, replica_id, 1, keepdims=False)
        source_targets = lax.dynamic_index_in_dim(targets, replica_id, 1, keepdims=False)
        source_positions = lax.dynamic_index_in_dim(positions, replica_id, 1, keepdims=False)
        scaled = (source_rows.astype(jnp.float32) * source_weights[..., None].astype(jnp.float32)).astype(jnp.bfloat16)
        slot_index = (micro_ids * SLOTS + source_ids * CAP + source_positions).astype(jnp.int32)
        slot_index = jnp.where(source_targets == expert_id, slot_index, N_MICRO * SLOTS).astype(jnp.int32)
        dispatched = jnp.zeros((N_MICRO * SLOTS, D_WIN), jnp.bfloat16)
        dispatched = dispatched.at[slot_index.reshape(-1)].set(scaled.reshape(-1, D_WIN), mode="drop")
        expert_hidden = lax.dynamic_index_in_dim(hidden_blocks, expert_id, 0, keepdims=False)
        hidden_block = lax.dynamic_index_in_dim(expert_hidden, replica_id, 0, keepdims=False)
        partial_value = jnp.dot(hidden_block.T, dispatched, preferred_element_type=jnp.float32)
        return partial_value.astype(jnp.bfloat16)

    def per_expert(expert_id):
        def add_copy(total, replica_id):
            return total + one_block(expert_id, replica_id).astype(jnp.float32), None

        total, unused = lax.scan(add_copy, jnp.zeros((FF, D_WIN), jnp.float32), jnp.arange(N_REPLICA, dtype=jnp.int32))
        return total

    return lax.map(per_expert, jnp.arange(EXPERTS, dtype=jnp.int32))
```

```python
import functools

import jax
import jax.numpy as jnp
from jax import lax
from jax.experimental import pallas as pl
from jax.experimental.pallas import tpu as pltpu
from jax.sharding import PartitionSpec as P

FIRST = 8
VMEM = 48 * 1024 * 1024


def iota(shape, dimension):
    return lax.broadcasted_iota(jnp.int32, shape, dimension)


def dispatch_kernel(capacity, parts, rows_ref, target_ref, weight_ref, out_ref):
    tokens, width = rows_ref.shape
    experts = out_ref.shape[0] // FIRST
    part = width // parts
    extra = capacity - FIRST
    target, weight = target_ref[...], weight_ref[...]
    member = iota((experts, tokens), 0) == target
    earlier = (iota((tokens, tokens), 0) < iota((tokens, tokens), 1)).astype(jnp.bfloat16)
    before = jnp.dot(member.astype(jnp.bfloat16), earlier, preferred_element_type=jnp.float32)
    position = jnp.sum(jnp.where(member, before, 0.0), axis=0, keepdims=True).astype(jnp.int32)
    row = iota((experts * FIRST, tokens), 0)
    expert, local = row // FIRST, row % FIRST
    mine = expert == target
    first = mine & (local == position)
    first_weight = jnp.sum(jnp.where(first, weight, 0.0), axis=1, keepdims=True)
    first = first.astype(jnp.bfloat16)
    for start in range(0, width, part):
        piece = jnp.dot(first, rows_ref[:, start : start + part], preferred_element_type=jnp.float32)
        out_ref[:, start : start + part] = (piece * first_weight).astype(jnp.bfloat16)
    late = mine & (FIRST + local % extra == position)
    late_weight = jnp.sum(jnp.where(late, weight, 0.0), axis=1, keepdims=True)
    total = jnp.zeros((experts * FIRST, part), jnp.float32)
    for q in range(parts):
        chosen = (late & (local // extra == q)).astype(jnp.bfloat16)
        total += jnp.dot(chosen, rows_ref[:, q * part : (q + 1) * part], preferred_element_type=jnp.float32)
    out_ref[:, width:] = (total * late_weight).astype(jnp.bfloat16)


def turn_kernel(groups, in_ref, out_ref):
    copies, rows, slots = out_ref.shape
    piece = rows // groups
    part = copies * piece
    turned = [
        in_ref[:, j * part : (j + 1) * part].astype(jnp.float32).T for j in range(groups)
    ]
    for r in range(copies):
        out_ref[r] = jnp.concatenate(
            [t[r * piece : (r + 1) * piece] for t in turned], axis=0
        ).astype(jnp.bfloat16)


def product_kernel(capacity, parts, moved_ref, hidden_ref, out_ref, total_ref):
    step = pl.program_id(0)
    copies, rows, slots = moved_ref.shape
    places = hidden_ref.shape[1]
    piece = rows // (parts + 1)
    extra = capacity - FIRST
    lane, place = iota((slots, places), 0), iota((slots, places), 1)
    sender, local = lane // FIRST, lane % FIRST
    first = (place == sender * capacity + local).astype(jnp.bfloat16)
    late = place == sender * capacity + FIRST + local % extra
    chosen = [(late & (local // extra == q)).astype(jnp.bfloat16) for q in range(parts)]

    @pl.when(step == 0)
    def _():
        total_ref[...] = jnp.zeros_like(total_ref)

    for r in range(copies):
        moved = moved_ref[r]
        behind = moved[parts * piece :]
        put = jnp.dot(moved[: parts * piece], first, preferred_element_type=jnp.float32)
        put += jnp.concatenate(
            [jnp.dot(behind, c, preferred_element_type=jnp.float32) for c in chosen], axis=0
        )
        total_ref[...] += jnp.dot(
            put.astype(jnp.bfloat16), hidden_ref[r], preferred_element_type=jnp.float32
        )

    @pl.when(step == pl.num_programs(0) - 1)
    def _():
        out_ref[...] = total_ref[...].astype(jnp.bfloat16)


def whole(shape):
    return pl.BlockSpec(shape, lambda *_: (0,) * len(shape))


def dispatch(rows, target, weight, experts, capacity, parts):
    tokens, width = rows.shape
    shape = (experts * FIRST, width + width // parts)
    return pl.pallas_call(
        functools.partial(dispatch_kernel, capacity, parts),
        out_shape=jax.ShapeDtypeStruct(shape, jnp.bfloat16),
        compiler_params=pltpu.CompilerParams(vmem_limit_bytes=VMEM),
        name="dispatch",
    )(rows, target.reshape(1, tokens), weight.reshape(1, tokens))


def turn(arrived, copies, parts):
    slots, width = arrived.shape
    return pl.pallas_call(
        functools.partial(turn_kernel, parts + 1),
        out_shape=jax.ShapeDtypeStruct((copies, width // copies, slots), jnp.bfloat16),
        compiler_params=pltpu.CompilerParams(vmem_limit_bytes=VMEM),
        name="turn",
    )(arrived)


def product(moved, hidden, capacity, parts):
    copies, rows, slots = moved.shape
    places, features = hidden.shape[1:]
    out = (rows // (parts + 1) * parts, features)
    block = 4
    return pl.pallas_call(
        functools.partial(product_kernel, capacity, parts),
        grid=(copies // block,),
        in_specs=[
            pl.BlockSpec((block, rows, slots), lambda i: (i, 0, 0)),
            pl.BlockSpec((block, places, features), lambda i: (i, 0, 0)),
        ],
        out_specs=whole(out),
        out_shape=jax.ShapeDtypeStruct(out, jnp.bfloat16),
        scratch_shapes=[pltpu.VMEM(out, jnp.float32)],
        compiler_params=pltpu.CompilerParams(vmem_limit_bytes=VMEM),
        name="product",
    )(moved, hidden)


def sum_over_micro(partial):
    size = 4
    me = lax.axis_index("micro")
    half = partial.shape[2] // 2
    ahead = [(i, (i + 1) % size) for i in range(size)]
    back = [(i, (i - 1) % size) for i in range(size)]

    def part(k):
        return lax.dynamic_index_in_dim(partial, (me + k) % size, 0, keepdims=False)

    def wide(v):
        return v.astype(jnp.float32)

    own, right, far, left = (part(k) for k in range(size))
    up = lax.ppermute(jnp.concatenate([far[:, :half], right[:, half:]], 1), "micro", ahead)
    down = lax.ppermute(jnp.concatenate([left[:, :half], far[:, half:]], 1), "micro", back)
    up_late = (wide(right[:, :half]) + wide(up[:, :half])).astype(partial.dtype)
    down_late = (wide(left[:, half:]) + wide(down[:, half:])).astype(partial.dtype)
    up_late = lax.ppermute(up_late, "micro", ahead)
    down_late = lax.ppermute(down_late, "micro", back)
    low = wide(own[:, :half]) + wide(up_late) + wide(down[:, :half])
    high = wide(own[:, half:]) + wide(up[:, half:]) + wide(down_late)
    return jnp.concatenate([low, high], 1).astype(partial.dtype)


def shards(grad_rows, routing, route_weight, saved_hidden):
    experts, copies, parts = (lax.axis_size(a) for a in ("expert", "replica", "micro"))
    places, features = saved_hidden.shape
    capacity = places // experts
    hidden = lax.all_gather(saved_hidden, "replica", axis=0, tiled=False)
    sent = dispatch(grad_rows, routing, route_weight, experts, capacity, parts)
    arrived = lax.all_to_all(
        sent.reshape(experts, FIRST, -1), "expert", split_axis=0, concat_axis=0, tiled=True
    )
    turned = turn(arrived.reshape(experts * FIRST, -1), copies, parts)
    moved = lax.all_to_all(turned, "replica", split_axis=0, concat_axis=0, tiled=True)
    partial = product(moved, hidden, capacity, parts)
    part = sum_over_micro(partial.reshape(parts, -1, features))
    piece = part.shape[0]
    out = part.reshape(piece, copies, features // copies).transpose(1, 0, 2)
    out = lax.all_to_all(out, "replica", split_axis=0, concat_axis=0, tiled=True)
    out = out.reshape(copies * piece, features // copies).T
    return out.astype(jnp.float32)[None]


def solution(mesh):
    rows = P(("expert", "replica", "micro"), None)
    return jax.shard_map(
        shards,
        mesh=mesh,
        in_specs=(rows, rows, rows, rows),
        out_specs=P("expert", "replica", "micro"),
        check_vma=False,
    )
```

```python
import functools

import jax
import jax.numpy as jnp
from jax import lax
from jax.experimental import pallas as pl
from jax.experimental.pallas import tpu as pltpu
from jax.sharding import Mesh
from jax.sharding import PartitionSpec as P

FIRST = 8
VMEM = 48 * 1024 * 1024


REPLICA = ("y", "x")


def iota(shape, dimension):
    return lax.broadcasted_iota(jnp.int32, shape, dimension)


def dispatch_kernel(capacity, parts, rows_ref, target_ref, weight_ref, out_ref):
    tokens, width = rows_ref.shape
    experts = out_ref.shape[0] // FIRST
    part = width // parts
    extra = capacity - FIRST
    target, weight = target_ref[...], weight_ref[...]
    member = iota((experts, tokens), 0) == target
    earlier = (iota((tokens, tokens), 0) < iota((tokens, tokens), 1)).astype(jnp.bfloat16)
    before = jnp.dot(member.astype(jnp.bfloat16), earlier, preferred_element_type=jnp.float32)
    position = jnp.sum(jnp.where(member, before, 0.0), axis=0, keepdims=True).astype(jnp.int32)
    row = iota((experts * FIRST, tokens), 0)
    expert, local = row // FIRST, row % FIRST
    mine = expert == target
    first = mine & (local == position)
    first_weight = jnp.sum(jnp.where(first, weight, 0.0), axis=1, keepdims=True)
    first = first.astype(jnp.bfloat16)
    for start in range(0, width, part):
        piece = jnp.dot(first, rows_ref[:, start : start + part], preferred_element_type=jnp.float32)
        out_ref[:, start : start + part] = (piece * first_weight).astype(jnp.bfloat16)
    late = mine & (FIRST + local % extra == position)
    late_weight = jnp.sum(jnp.where(late, weight, 0.0), axis=1, keepdims=True)
    total = jnp.zeros((experts * FIRST, part), jnp.float32)
    for q in range(parts):
        chosen = (late & (local // extra == q)).astype(jnp.bfloat16)
        total += jnp.dot(chosen, rows_ref[:, q * part : (q + 1) * part], preferred_element_type=jnp.float32)
    out_ref[:, width:] = (total * late_weight).astype(jnp.bfloat16)


def turn_kernel(groups, in_ref, out_ref):
    copies, rows, slots = out_ref.shape
    piece = rows // groups
    part = copies * piece
    turned = [
        in_ref[:, j * part : (j + 1) * part].astype(jnp.float32).T for j in range(groups)
    ]
    for r in range(copies):
        out_ref[r] = jnp.concatenate(
            [t[r * piece : (r + 1) * piece] for t in turned], axis=0
        ).astype(jnp.bfloat16)


def order_kernel(capacity, hidden_ref, out_ref):
    places = hidden_ref.shape[0]
    extra = capacity - FIRST
    senders = places // capacity
    row, place = iota((places, places), 0), iota((places, places), 1)
    late = row - senders * FIRST
    source = jnp.where(
        late < 0,
        row // FIRST * capacity + row % FIRST,
        late // extra * capacity + FIRST + late % extra,
    )
    chosen = (source == place).astype(jnp.bfloat16)
    out_ref[...] = jnp.dot(
        chosen, hidden_ref[...], preferred_element_type=jnp.float32
    ).astype(jnp.bfloat16)


def product_kernel(parts, extra, spot_ref, moved_ref, *refs):
    *hidden, out_ref = refs
    copies, rows, slots = moved_ref.shape
    side = hidden[0].shape[0]
    piece = rows // (parts + 1)
    senders = slots // FIRST
    lane, place = iota((slots, slots), 0), iota((slots, slots), 1)
    sender, local = lane // FIRST, lane % FIRST
    goes = [
        jnp.concatenate(
            [
                (local // extra == q) & (place == r * senders * extra + sender * extra + local % extra)
                for r in range(side)
            ],
            axis=0,
        ).astype(jnp.bfloat16)
        for q in range(parts)
    ]
    total = jnp.zeros(out_ref.shape, jnp.float32)
    for k in range(side):
        y = lax.rem(spot_ref[0] + k, side)
        moved = [moved_ref[y * side + lax.rem(spot_ref[1] + j, side)] for j in range(side)]
        behind = jnp.concatenate(
            [m[parts * piece :].astype(jnp.float32) for m in moved], axis=1
        ).astype(jnp.bfloat16)
        late = [jnp.dot(behind, g, preferred_element_type=jnp.float32) for g in goes]
        left = [m[: parts * piece] for m in moved]
        left.append(jnp.concatenate(late, axis=0).astype(jnp.bfloat16))
        if k == 2:
            low, high = hidden[2], hidden[3]
            cut = slots - low.shape[1]
            first = [part for j in range(side) for part in (low[j], high[j][:cut])]
            last = [high[j][cut:] for j in range(side)]
        else:
            held = hidden[k if k < 2 else k + 1]
            first = [held[j][:slots] for j in range(side)]
            last = [held[j][slots:] for j in range(side)]
        total += jnp.dot(
            jnp.concatenate(left, axis=1),
            jnp.concatenate(first + last, axis=0),
            preferred_element_type=jnp.float32,
        )
    out_ref[...] = total.astype(jnp.bfloat16)


def order(hidden, capacity):
    return pl.pallas_call(
        functools.partial(order_kernel, capacity),
        out_shape=jax.ShapeDtypeStruct(hidden.shape, jnp.bfloat16),
        compiler_params=pltpu.CompilerParams(vmem_limit_bytes=VMEM),
        name="order",
    )(hidden)


def dispatch(rows, target, weight, experts, capacity, parts):
    tokens, width = rows.shape
    shape = (experts * FIRST, width + width // parts)
    return pl.pallas_call(
        functools.partial(dispatch_kernel, capacity, parts),
        out_shape=jax.ShapeDtypeStruct(shape, jnp.bfloat16),
        compiler_params=pltpu.CompilerParams(vmem_limit_bytes=VMEM),
        name="dispatch",
    )(rows, target.reshape(1, tokens), weight.reshape(1, tokens))


def turn(arrived, copies, parts):
    slots, width = arrived.shape
    return pl.pallas_call(
        functools.partial(turn_kernel, parts + 1),
        out_shape=jax.ShapeDtypeStruct((copies, width // copies, slots), jnp.bfloat16),
        compiler_params=pltpu.CompilerParams(vmem_limit_bytes=VMEM),
        name="turn",
    )(arrived)


def product(moved, hidden, spot, capacity, parts):
    copies, rows, slots = moved.shape
    features = hidden[0].shape[2]
    out = (rows // (parts + 1) * parts, features)
    inside = pl.BlockSpec(memory_space=pltpu.VMEM)
    return pl.pallas_call(
        functools.partial(product_kernel, parts, capacity - FIRST),
        in_specs=[pl.BlockSpec(memory_space=pltpu.SMEM)] + [inside] * (1 + len(hidden)),
        out_specs=inside,
        out_shape=jax.ShapeDtypeStruct(out, jnp.bfloat16),
        compiler_params=pltpu.CompilerParams(vmem_limit_bytes=VMEM),
        name="product",
    )(spot, moved, *hidden)


def sum_over_micro(partial):
    size = 4
    me = lax.axis_index("micro")
    half = partial.shape[2] // 2
    ahead = [(i, (i + 1) % size) for i in range(size)]
    back = [(i, (i - 1) % size) for i in range(size)]

    def part(k):
        return lax.dynamic_index_in_dim(partial, (me + k) % size, 0, keepdims=False)

    def wide(v):
        return v.astype(jnp.float32)

    own, right, far, left = (part(k) for k in range(size))
    up = lax.ppermute(jnp.concatenate([far[:, :half], right[:, half:]], 1), "micro", ahead)
    down = lax.ppermute(jnp.concatenate([left[:, :half], far[:, half:]], 1), "micro", back)
    up_late = (wide(right[:, :half]) + wide(up[:, :half])).astype(partial.dtype)
    down_late = (wide(left[:, half:]) + wide(down[:, half:])).astype(partial.dtype)
    up_late = lax.ppermute(up_late, "micro", ahead)
    down_late = lax.ppermute(down_late, "micro", back)
    low = wide(own[:, :half]) + wide(up_late) + wide(down[:, :half])
    high = wide(own[:, half:]) + wide(up[:, half:]) + wide(down_late)
    return jnp.concatenate([low, high], 1).astype(partial.dtype)


def ring_gather(block, axis):
    size = lax.axis_size(axis)
    ahead = [(i, (i + 1) % size) for i in range(size)]
    back = [(i, (i - 1) % size) for i in range(size)]
    half = block.shape[-2] // 2
    behind = lax.ppermute(block, axis, ahead)
    before = lax.ppermute(block, axis, back)
    low = lax.ppermute(behind[..., :half, :], axis, ahead)
    high = lax.ppermute(before[..., half:, :], axis, back)
    return block, before, low, high, behind


def gather_hidden(block):
    own, before, low, high, behind = ring_gather(block, "x")
    row = jnp.stack([own, before, jnp.concatenate([low, high], axis=0), behind])
    return ring_gather(row, "y")


def shards(grad_rows, routing, route_weight, saved_hidden):
    experts, copies, parts = (lax.axis_size(a) for a in ("expert", REPLICA, "micro"))
    places, features = saved_hidden.shape
    capacity = places // experts
    hidden = order(saved_hidden, capacity)
    sent = dispatch(grad_rows, routing, route_weight, experts, capacity, parts)
    hidden = gather_hidden(hidden)
    arrived = lax.all_to_all(
        sent.reshape(experts, FIRST, -1), "expert", split_axis=0, concat_axis=0, tiled=True
    )
    turned = turn(arrived.reshape(experts * FIRST, -1), copies, parts)
    moved = lax.all_to_all(turned, REPLICA, split_axis=0, concat_axis=0, tiled=True)
    spot = jnp.stack([lax.axis_index("y"), lax.axis_index("x")])
    partial = product(moved, hidden, spot, capacity, parts)
    part = sum_over_micro(partial.reshape(parts, -1, features))
    piece = part.shape[0]
    out = part.reshape(piece, copies, features // copies).transpose(1, 0, 2)
    out = lax.all_to_all(out, REPLICA, split_axis=0, concat_axis=0, tiled=True)
    out = out.reshape(copies * piece, features // copies).T
    return out.astype(jnp.float32)[None]


def solution(mesh):
    experts, copies, parts = (mesh.shape[a] for a in ("expert", "replica", "micro"))
    side = 4
    split = Mesh(
        mesh.devices.reshape(experts, copies // side, side, parts), ("expert", "y", "x", "micro")
    )
    rows = P(("expert", "y", "x", "micro"), None)
    return jax.shard_map(
        shards,
        mesh=split,
        in_specs=(rows, rows, rows, rows),
        out_specs=P("expert", REPLICA, "micro"),
        check_vma=False,
    )
```

```python
import functools

import jax
import jax.numpy as jnp
from jax import lax
from jax.experimental import pallas as pl
from jax.experimental.pallas import tpu as pltpu
from jax.sharding import Mesh
from jax.sharding import PartitionSpec as P

FIRST = 8
VMEM = 48 * 1024 * 1024
WHOLE_VMEM = 60 * 1024 * 1024


REPLICA = ("y", "x")


def iota(shape, dimension):
    return lax.broadcasted_iota(jnp.int32, shape, dimension)


def dispatch_kernel(capacity, parts, rows_ref, target_ref, weight_ref, out_ref):
    tokens, width = rows_ref.shape
    experts = out_ref.shape[0] // FIRST
    part = width // parts
    extra = capacity - FIRST
    target, weight = target_ref[...], weight_ref[...]
    member = iota((experts, tokens), 0) == target
    earlier = (iota((tokens, tokens), 0) < iota((tokens, tokens), 1)).astype(jnp.bfloat16)
    before = jnp.dot(member.astype(jnp.bfloat16), earlier, preferred_element_type=jnp.float32)
    position = jnp.sum(jnp.where(member, before, 0.0), axis=0, keepdims=True).astype(jnp.int32)
    row = iota((experts * FIRST, tokens), 0)
    expert, local = row // FIRST, row % FIRST
    mine = expert == target
    first = mine & (local == position)
    first_weight = jnp.sum(jnp.where(first, weight, 0.0), axis=1, keepdims=True)
    first = first.astype(jnp.bfloat16)
    for start in range(0, width, part):
        piece = jnp.dot(first, rows_ref[:, start : start + part], preferred_element_type=jnp.float32)
        out_ref[:, start : start + part] = (piece * first_weight).astype(jnp.bfloat16)
    late = mine & (FIRST + local % extra == position)
    late_weight = jnp.sum(jnp.where(late, weight, 0.0), axis=1, keepdims=True)
    total = jnp.zeros((experts * FIRST, part), jnp.float32)
    for q in range(parts):
        chosen = (late & (local // extra == q)).astype(jnp.bfloat16)
        total += jnp.dot(chosen, rows_ref[:, q * part : (q + 1) * part], preferred_element_type=jnp.float32)
    out_ref[:, width:] = (total * late_weight).astype(jnp.bfloat16)


def turn_kernel(groups, in_ref, out_ref):
    copies, rows, slots = out_ref.shape
    piece = rows // groups
    part = copies * piece
    turned = [
        in_ref[:, j * part : (j + 1) * part].astype(jnp.float32).T for j in range(groups)
    ]
    for r in range(copies):
        out_ref[r] = jnp.concatenate(
            [t[r * piece : (r + 1) * piece] for t in turned], axis=0
        ).astype(jnp.bfloat16)


def order_kernel(capacity, *refs):
    own_ref, before_ref, low_ref, high_ref, behind_ref, out_ref = refs
    places = own_ref.shape[0]
    extra = capacity - FIRST
    senders = places // capacity
    row, place = iota((places, places), 0), iota((places, places), 1)
    late = row - senders * FIRST
    source = jnp.where(
        late < 0,
        row // FIRST * capacity + row % FIRST,
        late // extra * capacity + FIRST + late % extra,
    )
    chosen = (source == place).astype(jnp.bfloat16)
    far = jnp.concatenate([low_ref[...], high_ref[...]], axis=0)
    for i, block in enumerate((own_ref[...], before_ref[...], far, behind_ref[...])):
        out_ref[i] = jnp.dot(chosen, block, preferred_element_type=jnp.float32).astype(jnp.bfloat16)


def product_kernel(parts, extra, far, spot_ref, moved_ref, *refs):
    *hidden, out_ref = refs
    copies, rows, slots = moved_ref.shape
    side = hidden[0].shape[0]
    piece = rows // (parts + 1)
    senders = slots // FIRST
    lane, place = iota((slots, slots), 0), iota((slots, slots), 1)
    sender, local = lane // FIRST, lane % FIRST
    goes = [
        jnp.concatenate(
            [
                (local // extra == q) & (place == r * senders * extra + sender * extra + local % extra)
                for r in range(side)
            ],
            axis=0,
        ).astype(jnp.bfloat16)
        for q in range(parts)
    ]
    total = None
    for k, *held in [(2, *hidden[:2])] if far else [(0, hidden[0]), (1, hidden[1]), (3, hidden[2])]:
        y = lax.rem(spot_ref[0] + k, side)
        moved = [moved_ref[y * side + lax.rem(spot_ref[1] + j, side)] for j in range(side)]
        behind = jnp.concatenate(
            [m[parts * piece :].astype(jnp.float32) for m in moved], axis=1
        ).astype(jnp.bfloat16)
        late = [jnp.dot(behind, g, preferred_element_type=jnp.float32) for g in goes]
        left = [m[: parts * piece] for m in moved]
        left.append(jnp.concatenate(late, axis=0).astype(jnp.bfloat16))
        first, last = [], []
        for j in range(side):
            *whole, end = [h[j] for h in held]
            cut = slots - sum(w.shape[0] for w in whole)
            first += [*whole, end[:cut]]
            last.append(end[cut:])
        product = jnp.dot(
            jnp.concatenate(left, axis=1),
            jnp.concatenate(first + last, axis=0),
            preferred_element_type=jnp.float32,
        )
        total = product if total is None else total + product
    if far:
        total += hidden[2][...]
    out_ref[...] = total.astype(out_ref.dtype)


def order(blocks, capacity):
    return pl.pallas_call(
        functools.partial(order_kernel, capacity),
        out_shape=jax.ShapeDtypeStruct((4, *blocks[0].shape), jnp.bfloat16),
        compiler_params=pltpu.CompilerParams(vmem_limit_bytes=VMEM),
        name="order",
    )(*blocks)


def dispatch(rows, target, weight, experts, capacity, parts):
    tokens, width = rows.shape
    shape = (experts * FIRST, width + width // parts)
    return pl.pallas_call(
        functools.partial(dispatch_kernel, capacity, parts),
        out_shape=jax.ShapeDtypeStruct(shape, jnp.bfloat16),
        compiler_params=pltpu.CompilerParams(vmem_limit_bytes=WHOLE_VMEM),
        name="dispatch",
    )(rows, target.reshape(1, tokens), weight.reshape(1, tokens))


def turn(arrived, copies, parts):
    slots, width = arrived.shape
    return pl.pallas_call(
        functools.partial(turn_kernel, parts + 1),
        out_shape=jax.ShapeDtypeStruct((copies, width // copies, slots), jnp.bfloat16),
        compiler_params=pltpu.CompilerParams(vmem_limit_bytes=VMEM),
        name="turn",
    )(arrived)


def product(moved, hidden, spot, capacity, parts):
    copies, rows, slots = moved.shape
    features = hidden[0].shape[2]
    out = (rows // (parts + 1) * parts, features)
    inside = pl.BlockSpec(memory_space=pltpu.VMEM)

    def call(far, blocks, kind):
        return pl.pallas_call(
            functools.partial(product_kernel, parts, capacity - FIRST, far),
            in_specs=[pl.BlockSpec(memory_space=pltpu.SMEM)] + [inside] * (1 + len(blocks)),
            out_specs=inside,
            out_shape=jax.ShapeDtypeStruct(out, kind),
            compiler_params=pltpu.CompilerParams(vmem_limit_bytes=VMEM),
            name="far_product" if far else "near_product",
        )(spot, moved, *blocks)

    own, before, low, high, behind = hidden
    near = call(False, (own, before, behind), jnp.float32)
    return call(True, (low, high, near), jnp.bfloat16)


def sum_over_micro(partial):
    size = 4
    me = lax.axis_index("micro")
    half = partial.shape[2] // 2
    ahead = [(i, (i + 1) % size) for i in range(size)]
    back = [(i, (i - 1) % size) for i in range(size)]

    def part(k):
        return lax.dynamic_index_in_dim(partial, (me + k) % size, 0, keepdims=False)

    def wide(v):
        return v.astype(jnp.float32)

    own, right, far, left = (part(k) for k in range(size))
    up = lax.ppermute(jnp.concatenate([far[:, :half], right[:, half:]], 1), "micro", ahead)
    down = lax.ppermute(jnp.concatenate([left[:, :half], far[:, half:]], 1), "micro", back)
    up_late = (wide(right[:, :half]) + wide(up[:, :half])).astype(partial.dtype)
    down_late = (wide(left[:, half:]) + wide(down[:, half:])).astype(partial.dtype)
    up_late = lax.ppermute(up_late, "micro", ahead)
    down_late = lax.ppermute(down_late, "micro", back)
    low = wide(own[:, :half]) + wide(up_late) + wide(down[:, :half])
    high = wide(own[:, half:]) + wide(up[:, half:]) + wide(down_late)
    return jnp.concatenate([low, high], 1).astype(partial.dtype)


def ring_gather(block, axis):
    size = lax.axis_size(axis)
    ahead = [(i, (i + 1) % size) for i in range(size)]
    back = [(i, (i - 1) % size) for i in range(size)]
    half = block.shape[-2] // 2
    behind = lax.ppermute(block, axis, ahead)
    before = lax.ppermute(block, axis, back)
    low = lax.ppermute(behind[..., :half, :], axis, ahead)
    high = lax.ppermute(before[..., half:, :], axis, back)
    return block, before, low, high, behind


def gather_hidden(block, capacity):
    return ring_gather(order(ring_gather(block, "x"), capacity), "y")


def shards(grad_rows, routing, route_weight, saved_hidden):
    experts, copies, parts = (lax.axis_size(a) for a in ("expert", REPLICA, "micro"))
    places, features = saved_hidden.shape
    capacity = places // experts
    sent = dispatch(grad_rows, routing, route_weight, experts, capacity, parts)
    hidden = gather_hidden(saved_hidden, capacity)
    arrived = lax.all_to_all(
        sent.reshape(experts, FIRST, -1), "expert", split_axis=0, concat_axis=0, tiled=True
    )
    turned = turn(arrived.reshape(experts * FIRST, -1), copies, parts)
    moved = lax.all_to_all(turned, REPLICA, split_axis=0, concat_axis=0, tiled=True)
    spot = jnp.stack([lax.axis_index("y"), lax.axis_index("x")])
    partial = product(moved, hidden, spot, capacity, parts)
    part = sum_over_micro(partial.reshape(parts, -1, features))
    piece = part.shape[0]
    out = part.reshape(piece, copies, features // copies).transpose(1, 0, 2)
    out = lax.all_to_all(out, REPLICA, split_axis=0, concat_axis=0, tiled=True)
    out = out.reshape(copies * piece, features // copies).T
    return out.astype(jnp.float32)[None]


def solution(mesh):
    experts, copies, parts = (mesh.shape[a] for a in ("expert", "replica", "micro"))
    side = 4
    split = Mesh(
        mesh.devices.reshape(experts, copies // side, side, parts), ("expert", "y", "x", "micro")
    )
    rows = P(("expert", "y", "x", "micro"), None)
    return jax.shard_map(
        shards,
        mesh=split,
        in_specs=(rows, rows, rows, rows),
        out_specs=P("expert", REPLICA, "micro"),
        check_vma=False,
    )
```

```python
import functools
import math

import jax
import jax.numpy as jnp
from jax import lax
from jax.experimental import pallas as pl
from jax.experimental.pallas import tpu as pltpu
from jax.sharding import Mesh
from jax.sharding import PartitionSpec as P

FIRST = 8
VMEM = 48 * 1024 * 1024
WHOLE_VMEM = 60 * 1024 * 1024


REPLICA = ("y", "x")


def iota(shape, dimension):
    return lax.broadcasted_iota(jnp.int32, shape, dimension)


def dispatch_kernel(capacity, parts, rows_ref, target_ref, weight_ref, out_ref):
    tokens, width = rows_ref.shape
    experts = out_ref.shape[0] // FIRST
    part = width // parts
    extra = capacity - FIRST
    target, weight = target_ref[...], weight_ref[...]
    member = iota((experts, tokens), 0) == target
    earlier = (iota((tokens, tokens), 0) < iota((tokens, tokens), 1)).astype(jnp.bfloat16)
    before = jnp.dot(member.astype(jnp.bfloat16), earlier, preferred_element_type=jnp.float32)
    position = jnp.sum(jnp.where(member, before, 0.0), axis=0, keepdims=True).astype(jnp.int32)
    row = iota((experts * FIRST, tokens), 0)
    expert, local = row // FIRST, row % FIRST
    mine = expert == target
    first = mine & (local == position)
    first_weight = jnp.sum(jnp.where(first, weight, 0.0), axis=1, keepdims=True)
    first = first.astype(jnp.bfloat16)
    for start in range(0, width, part):
        piece = jnp.dot(first, rows_ref[:, start : start + part], preferred_element_type=jnp.float32)
        out_ref[:, start : start + part] = (piece * first_weight).astype(jnp.bfloat16)
    late = mine & (FIRST + local % extra == position)
    late_weight = jnp.sum(jnp.where(late, weight, 0.0), axis=1, keepdims=True)
    total = jnp.zeros((experts * FIRST, part), jnp.float32)
    for q in range(parts):
        chosen = (late & (local // extra == q)).astype(jnp.bfloat16)
        total += jnp.dot(chosen, rows_ref[:, q * part : (q + 1) * part], preferred_element_type=jnp.float32)
    out_ref[:, width:] = (total * late_weight).astype(jnp.bfloat16)


def turn_kernel(groups, in_ref, out_ref):
    copies, rows, slots = out_ref.shape
    piece = rows // groups
    part = copies * piece
    turned = [
        in_ref[:, j * part : (j + 1) * part].astype(jnp.float32).T for j in range(groups)
    ]
    for r in range(copies):
        out_ref[r] = jnp.concatenate(
            [t[r * piece : (r + 1) * piece] for t in turned], axis=0
        ).astype(jnp.bfloat16)


def order_kernel(capacity, *refs):
    *blocks, out_ref = refs
    places = out_ref.shape[1]
    extra = capacity - FIRST
    senders = places // capacity
    row, place = iota((places, places), 0), iota((places, places), 1)
    late = row - senders * FIRST
    source = jnp.where(
        late < 0,
        row // FIRST * capacity + row % FIRST,
        late // extra * capacity + FIRST + late % extra,
    )
    chosen = (source == place).astype(jnp.bfloat16)
    for i, block in enumerate(blocks):
        out_ref[i] = jnp.dot(
            chosen, block[...], preferred_element_type=jnp.float32
        ).astype(jnp.bfloat16)


def product_kernel(parts, extra, far, spot_ref, moved_ref, *refs):
    *hidden, out_ref = refs
    copies, rows, slots = moved_ref.shape
    side = math.isqrt(copies)
    piece = rows // (parts + 1)
    senders = slots // FIRST
    lane, place = iota((slots, slots), 0), iota((slots, slots), 1)
    sender, local = lane // FIRST, lane % FIRST
    goes = [
        jnp.concatenate(
            [
                (local // extra == q) & (place == r * senders * extra + sender * extra + local % extra)
                for r in range(side)
            ],
            axis=0,
        ).astype(jnp.bfloat16)
        for q in range(parts)
    ]
    total = None
    for k, held in [(2, hidden[0])] if far else [(0, hidden[0]), (1, hidden[1]), (3, hidden[2])]:
        y = lax.rem(spot_ref[0] + k * spot_ref[2], side)
        moved = [moved_ref[y * side + lax.rem(spot_ref[1] + j * spot_ref[2], side)] for j in range(side)]
        behind = jnp.concatenate(
            [m[parts * piece :].astype(jnp.float32) for m in moved], axis=1
        ).astype(jnp.bfloat16)
        late = [jnp.dot(behind, g, preferred_element_type=jnp.float32) for g in goes]
        left = [m[: parts * piece] for m in moved]
        left.append(jnp.concatenate(late, axis=0).astype(jnp.bfloat16))
        first = [held[j][:slots] for j in range(side)]
        last = [held[j][slots:] for j in range(side)]
        product = jnp.dot(
            jnp.concatenate(left, axis=1),
            jnp.concatenate(first + last, axis=0),
            preferred_element_type=jnp.float32,
        )
        total = product if total is None else total + product
    if far:
        total += hidden[1][...]
    out_ref[...] = total.astype(out_ref.dtype)


def order(blocks, capacity):
    return pl.pallas_call(
        functools.partial(order_kernel, capacity),
        out_shape=jax.ShapeDtypeStruct((4, *blocks[0].shape), jnp.bfloat16),
        compiler_params=pltpu.CompilerParams(vmem_limit_bytes=VMEM),
        name="order",
    )(*blocks)


def dispatch(rows, target, weight, experts, capacity, parts):
    tokens, width = rows.shape
    shape = (experts * FIRST, width + width // parts)
    return pl.pallas_call(
        functools.partial(dispatch_kernel, capacity, parts),
        out_shape=jax.ShapeDtypeStruct(shape, jnp.bfloat16),
        compiler_params=pltpu.CompilerParams(vmem_limit_bytes=WHOLE_VMEM),
        name="dispatch",
    )(rows, target.reshape(1, tokens), weight.reshape(1, tokens))


def turn(arrived, copies, parts):
    slots, width = arrived.shape
    return pl.pallas_call(
        functools.partial(turn_kernel, parts + 1),
        out_shape=jax.ShapeDtypeStruct((copies, width // copies, slots), jnp.bfloat16),
        compiler_params=pltpu.CompilerParams(vmem_limit_bytes=VMEM),
        name="turn",
    )(arrived)


def product(moved, hidden, spot, capacity, parts):
    copies, rows, slots = moved.shape
    features = hidden[0].shape[2]
    out = (rows // (parts + 1) * parts, features)
    inside = pl.BlockSpec(memory_space=pltpu.VMEM)

    def call(far, blocks, kind):
        return pl.pallas_call(
            functools.partial(product_kernel, parts, capacity - FIRST, far),
            in_specs=[pl.BlockSpec(memory_space=pltpu.SMEM)] + [inside] * (1 + len(blocks)),
            out_specs=inside,
            out_shape=jax.ShapeDtypeStruct(out, kind),
            compiler_params=pltpu.CompilerParams(vmem_limit_bytes=VMEM),
            name="far_product" if far else "near_product",
        )(spot, moved, *blocks)

    own, one_back, two_back, three_back = hidden
    near = call(False, (own, one_back, three_back), jnp.float32)
    return call(True, (two_back, near), jnp.bfloat16)


def way():
    return 1 - 2 * (lax.axis_index("expert") % 2)


def step(block, axis, steps):
    size, experts = lax.axis_size(axis), lax.axis_size("expert")
    perm = [
        (e * size + i, e * size + (i + steps * (1 - 2 * (e % 2))) % size)
        for e in range(experts)
        for i in range(size)
    ]
    return lax.ppermute(block, ("expert", axis), perm)


def sum_over_micro(partial):
    me, size = lax.axis_index("micro"), lax.axis_size("micro")

    def part(steps):
        place = (me + way() * steps + size) % size
        return lax.dynamic_index_in_dim(partial, place, 0, keepdims=False)

    def wide(v):
        return v.astype(jnp.float32)

    came = step(part(2), "micro", 1)
    direct = step(part(-1), "micro", -1)
    late = step((wide(part(1)) + wide(came)).astype(partial.dtype), "micro", 1)
    return (wide(part(0)) + wide(direct) + wide(late)).astype(partial.dtype)


def ring_gather(block, axis):
    one_back = step(block, axis, 1)
    three_back = step(block, axis, -1)
    two_back = step(one_back, axis, 1)
    return block, one_back, two_back, three_back


def gather_hidden(block, capacity):
    return ring_gather(order(ring_gather(block, "x"), capacity), "y")


def shards(grad_rows, routing, route_weight, saved_hidden):
    experts, copies, parts = (lax.axis_size(a) for a in ("expert", REPLICA, "micro"))
    places, features = saved_hidden.shape
    capacity = places // experts
    sent = dispatch(grad_rows, routing, route_weight, experts, capacity, parts)
    hidden = gather_hidden(saved_hidden, capacity)
    arrived = lax.all_to_all(
        sent.reshape(experts, FIRST, -1), "expert", split_axis=0, concat_axis=0, tiled=True
    )
    turned = turn(arrived.reshape(experts * FIRST, -1), copies, parts)
    moved = lax.all_to_all(turned, REPLICA, split_axis=0, concat_axis=0, tiled=True)
    spot = jnp.stack([lax.axis_index("y"), lax.axis_index("x"), 4 - way()])
    partial = product(moved, hidden, spot, capacity, parts)
    part = sum_over_micro(partial.reshape(parts, -1, features))
    piece = part.shape[0]
    out = part.reshape(piece, copies, features // copies).transpose(1, 0, 2)
    out = lax.all_to_all(out, REPLICA, split_axis=0, concat_axis=0, tiled=True)
    out = out.reshape(copies * piece, features // copies).T
    return out.astype(jnp.float32)[None]


def solution(mesh):
    experts, copies, parts = (mesh.shape[a] for a in ("expert", "replica", "micro"))
    side = 4
    split = Mesh(
        mesh.devices.reshape(experts, copies // side, side, parts), ("expert", "y", "x", "micro")
    )
    rows = P(("expert", "y", "x", "micro"), None)
    return jax.shard_map(
        shards,
        mesh=split,
        in_specs=(rows, rows, rows, rows),
        out_specs=P("expert", REPLICA, "micro"),
        check_vma=False,
    )
```

```python
import functools
import math

import jax
import jax.numpy as jnp
from jax import lax
from jax.experimental import pallas as pl
from jax.experimental.pallas import tpu as pltpu
from jax.sharding import Mesh
from jax.sharding import PartitionSpec as P

FIRST = 8
VMEM = 48 * 1024 * 1024
WHOLE_VMEM = 60 * 1024 * 1024


REPLICA = ("y", "x")


def iota(shape, dimension):
    return lax.broadcasted_iota(jnp.int32, shape, dimension)


def dispatch_kernel(capacity, parts, rows_ref, target_ref, weight_ref, out_ref):
    tokens, width = rows_ref.shape
    experts = out_ref.shape[0] // FIRST
    part = width // parts
    extra = capacity - FIRST
    target, weight = target_ref[...], weight_ref[...]
    member = iota((experts, tokens), 0) == target
    earlier = (iota((tokens, tokens), 0) < iota((tokens, tokens), 1)).astype(jnp.bfloat16)
    before = jnp.dot(member.astype(jnp.bfloat16), earlier, preferred_element_type=jnp.float32)
    position = jnp.sum(jnp.where(member, before, 0.0), axis=0, keepdims=True).astype(jnp.int32)
    row = iota((experts * FIRST, tokens), 0)
    expert, local = row // FIRST, row % FIRST
    mine = expert == target
    first = mine & (local == position)
    first_weight = jnp.sum(jnp.where(first, weight, 0.0), axis=1, keepdims=True)
    first = first.astype(jnp.bfloat16)
    for start in range(0, width, part):
        piece = jnp.dot(first, rows_ref[:, start : start + part], preferred_element_type=jnp.float32)
        out_ref[:, start : start + part] = (piece * first_weight).astype(jnp.bfloat16)
    late = mine & (FIRST + local % extra == position)
    late_weight = jnp.sum(jnp.where(late, weight, 0.0), axis=1, keepdims=True)
    total = jnp.zeros((experts * FIRST, part), jnp.float32)
    for q in range(parts):
        chosen = (late & (local // extra == q)).astype(jnp.bfloat16)
        total += jnp.dot(chosen, rows_ref[:, q * part : (q + 1) * part], preferred_element_type=jnp.float32)
    out_ref[:, width:] = (total * late_weight).astype(jnp.bfloat16)


def turn_kernel(groups, in_ref, out_ref):
    copies, rows, slots = out_ref.shape
    piece = rows // groups
    part = copies * piece
    turned = [
        in_ref[:, j * part : (j + 1) * part].astype(jnp.float32).T for j in range(groups)
    ]
    for r in range(copies):
        out_ref[r] = jnp.concatenate(
            [t[r * piece : (r + 1) * piece] for t in turned], axis=0
        ).astype(jnp.bfloat16)


def order_kernel(capacity, *refs):
    *blocks, out_ref = refs
    places = out_ref.shape[1]
    extra = capacity - FIRST
    senders = places // capacity
    row, place = iota((places, places), 0), iota((places, places), 1)
    late = row - senders * FIRST
    source = jnp.where(
        late < 0,
        row // FIRST * capacity + row % FIRST,
        late // extra * capacity + FIRST + late % extra,
    )
    chosen = (source == place).astype(jnp.bfloat16)
    for i, block in enumerate(blocks):
        out_ref[i] = jnp.dot(
            chosen, block[...], preferred_element_type=jnp.float32
        ).astype(jnp.bfloat16)


def product_kernel(parts, extra, spot_ref, moved_ref, *refs):
    *hidden, out_ref = refs
    copies, rows, slots = moved_ref.shape
    side = math.isqrt(copies)
    piece = rows // (parts + 1)
    senders = slots // FIRST
    lane, place = iota((slots, slots), 0), iota((slots, slots), 1)
    sender, local = lane // FIRST, lane % FIRST
    goes = [
        jnp.concatenate(
            [
                (local // extra == q) & (place == r * senders * extra + sender * extra + local % extra)
                for r in range(side)
            ],
            axis=0,
        ).astype(jnp.bfloat16)
        for q in range(parts)
    ]
    total = None
    for k, held in enumerate(hidden):
        y = lax.rem(spot_ref[0] + k * spot_ref[2], side)
        moved = [moved_ref[y * side + lax.rem(spot_ref[1] + j * spot_ref[2], side)] for j in range(side)]
        behind = jnp.concatenate(
            [m[parts * piece :].astype(jnp.float32) for m in moved], axis=1
        ).astype(jnp.bfloat16)
        late = [jnp.dot(behind, g, preferred_element_type=jnp.float32) for g in goes]
        left = [m[: parts * piece] for m in moved]
        left.append(jnp.concatenate(late, axis=0).astype(jnp.bfloat16))
        first = [held[j][:slots] for j in range(side)]
        last = [held[j][slots:] for j in range(side)]
        product = jnp.dot(
            jnp.concatenate(left, axis=1),
            jnp.concatenate(first + last, axis=0),
            preferred_element_type=jnp.float32,
        )
        total = product if total is None else total + product
    out_ref[...] = total.astype(out_ref.dtype)


def order(blocks, capacity):
    return pl.pallas_call(
        functools.partial(order_kernel, capacity),
        out_shape=jax.ShapeDtypeStruct((4, *blocks[0].shape), jnp.bfloat16),
        compiler_params=pltpu.CompilerParams(vmem_limit_bytes=VMEM),
        name="order",
    )(*blocks)


def dispatch(rows, target, weight, experts, capacity, parts):
    tokens, width = rows.shape
    shape = (experts * FIRST, width + width // parts)
    return pl.pallas_call(
        functools.partial(dispatch_kernel, capacity, parts),
        out_shape=jax.ShapeDtypeStruct(shape, jnp.bfloat16),
        compiler_params=pltpu.CompilerParams(vmem_limit_bytes=WHOLE_VMEM),
        name="dispatch",
    )(rows, target.reshape(1, tokens), weight.reshape(1, tokens))


def turn(arrived, copies, parts):
    slots, width = arrived.shape
    return pl.pallas_call(
        functools.partial(turn_kernel, parts + 1),
        out_shape=jax.ShapeDtypeStruct((copies, width // copies, slots), jnp.bfloat16),
        compiler_params=pltpu.CompilerParams(vmem_limit_bytes=VMEM),
        name="turn",
    )(arrived)


def product(moved, hidden, spot, capacity, parts):
    copies, rows, slots = moved.shape
    features = hidden[0].shape[2]
    out = (rows // (parts + 1) * parts, features)
    inside = pl.BlockSpec(memory_space=pltpu.VMEM)

    return pl.pallas_call(
        functools.partial(product_kernel, parts, capacity - FIRST),
        in_specs=[pl.BlockSpec(memory_space=pltpu.SMEM)] + [inside] * (1 + len(hidden)),
        out_specs=inside,
        out_shape=jax.ShapeDtypeStruct(out, jnp.bfloat16),
        compiler_params=pltpu.CompilerParams(vmem_limit_bytes=VMEM),
        name="product",
    )(spot, moved, *hidden)


def way():
    return 1 - 2 * (lax.axis_index("expert") % 2)


def step(block, axis, steps):
    size, experts = lax.axis_size(axis), lax.axis_size("expert")
    perm = [
        (e * size + i, e * size + (i + steps * (1 - 2 * (e % 2))) % size)
        for e in range(experts)
        for i in range(size)
    ]
    return lax.ppermute(block, ("expert", axis), perm)


def sum_over_micro(partial):
    me, size = lax.axis_index("micro"), lax.axis_size("micro")

    def part(steps):
        place = (me + way() * steps + size) % size
        return lax.dynamic_index_in_dim(partial, place, 0, keepdims=False)

    def wide(v):
        return v.astype(jnp.float32)

    came = step(part(2), "micro", 1)
    direct = step(part(-1), "micro", -1)
    late = step((wide(part(1)) + wide(came)).astype(partial.dtype), "micro", 1)
    return (wide(part(0)) + wide(direct) + wide(late)).astype(partial.dtype)


def ring_gather(block, axis):
    one_back = step(block, axis, 1)
    three_back = step(block, axis, -1)
    two_back = step(one_back, axis, 1)
    return block, one_back, two_back, three_back


def gather_hidden(block, capacity):
    return ring_gather(order(ring_gather(block, "x"), capacity), "y")


def shards(grad_rows, routing, route_weight, saved_hidden):
    experts, copies, parts = (lax.axis_size(a) for a in ("expert", REPLICA, "micro"))
    places, features = saved_hidden.shape
    capacity = places // experts
    sent = dispatch(grad_rows, routing, route_weight, experts, capacity, parts)
    hidden = gather_hidden(saved_hidden, capacity)
    arrived = lax.all_to_all(
        sent.reshape(experts, FIRST, -1), "expert", split_axis=0, concat_axis=0, tiled=True
    )
    turned = turn(arrived.reshape(experts * FIRST, -1), copies, parts)
    moved = lax.all_to_all(turned, REPLICA, split_axis=0, concat_axis=0, tiled=True)
    spot = jnp.stack([lax.axis_index("y"), lax.axis_index("x"), 4 - way()])
    partial = product(moved, hidden, spot, capacity, parts)
    part = sum_over_micro(partial.reshape(parts, -1, features))
    piece = part.shape[0]
    out = part.reshape(piece, copies, features // copies).transpose(1, 0, 2)
    out = lax.all_to_all(out, REPLICA, split_axis=0, concat_axis=0, tiled=True)
    out = out.reshape(copies * piece, features // copies).T
    return out.astype(jnp.float32)[None]


def solution(mesh):
    experts, copies, parts = (mesh.shape[a] for a in ("expert", "replica", "micro"))
    side = 4
    split = Mesh(
        mesh.devices.reshape(experts, copies // side, side, parts), ("expert", "y", "x", "micro")
    )
    rows = P(("expert", "y", "x", "micro"), None)
    return jax.shard_map(
        shards,
        mesh=split,
        in_specs=(rows, rows, rows, rows),
        out_specs=P("expert", REPLICA, "micro"),
        check_vma=False,
    )
```
